256 devices in a mesh: blk: 8 (over x_hi, y), wide: 32 (over x_lo, z, core).
Axes of the slice: x: 4 (x_hi: 2, x_lo: 2; x = x_hi * 2 + x_lo), y: 4, z: 8, core: 2. Of those that a mesh axis runs over, the one named last changes fastest.
Arguments:
- users: bfloat16 [1048576, 256], P(('blk', 'wide')), may hold values from -1.5 to 1.5
- items: bfloat16 [131072, 256], P(('blk', 'wide')), may hold values from -1.5 to 1.5
- user_pairs: int32 [256, 8, 16], P(('blk', 'wide')), may hold values from 0 to 127, as said below
- user_ratings: bfloat16 [256, 8, 16, 128, 128], P(('blk', 'wide')), may hold values from 0 to 5, as said below
- user_counts: int32 [256, 8], P(('blk', 'wide')), may hold values from 1 to 16
- item_pairs: int32 [256, 128], P(('blk', 'wide')), may hold values from 0 to 127, as said below
- item_ratings: bfloat16 [256, 128, 128, 128], P(('blk', 'wide')), may hold values from 0 to 5, as said below
- live_item_counts: int32 [256], P(('blk', 'wide')), may hold values from 1 to 128
Outputs:
- new_users: bfloat16 [1048576, 256], P(('blk', 'wide'))
- new_items: bfloat16 [131072, 256], P(('blk', 'wide'))
The draws below stay inside these ranges and needn't reach their ends.
Inputs may be any that keep to these rules, and one draw needn't show every extreme that they name: `user_pairs`: within one group and slice the slots name distinct pairs; p // 4 is the user block, p % (4) the item block. `user_ratings`: 0 marks an unobserved rating; observed ratings lie in 1 to 5. `item_pairs`: within one group the slots name distinct pairs; p // 32 is the item block, p % (32) the relaid user block. `item_ratings`: 0 marks an unobserved rating; observed ratings lie in 1 to 5.
All inputs are finite; a program needn't handle non-finite values.
Results may differ from the reference program's by a relative error of at most 0.0044.
Values may be sent and summed in bfloat16 or wider, within the bound.
A program may use at most 128 MiB of HBM per device.

```python
import math
import jax
import jax.numpy as jnp
from jax import lax

R = 256
B = 128
UD = 4096
ID = 512
CAP = 16
ICAP = 128
NUSERS = 1048576
NITEMS = 131072
N_BLK = 8
N_WIDE = 32
DEVICES = 256


def pick_pairs(key, row_count, keep_count, pair_count):
    key_list = jax.random.split(key, row_count)
    shuffled = jax.vmap(lambda sub_key: jax.random.permutation(sub_key, pair_count))(key_list)
    shuffled = shuffled.astype(jnp.int32)
    top_row = jax.random.randint(jax.random.fold_in(key, 7), (), 0, row_count)
    low_row = (top_row + 1) % row_count
    positions = jnp.arange(pair_count, dtype=jnp.int32)
    lead_top = jnp.argmax(shuffled == pair_count - 1, axis=1).astype(jnp.int32)
    lead_low = jnp.argmax(shuffled == 0, axis=1).astype(jnp.int32)
    rolled_top = jnp.take_along_axis(shuffled, (positions[None, :] + lead_top[:, None]) % pair_count, axis=1)
    rolled_low = jnp.take_along_axis(shuffled, (positions[None, :] + lead_low[:, None]) % pair_count, axis=1)
    row_ids = jnp.arange(row_count, dtype=jnp.int32)[:, None]
    shuffled = jnp.where(row_ids == top_row, rolled_top, shuffled)
    shuffled = jnp.where(row_ids == low_row, rolled_low, shuffled)
    return shuffled[:, :keep_count]


def pick_counts(key, array_shape, upper_count):
    cell_count = math.prod(array_shape)
    busy_key, base_key, spot_key = jax.random.split(key, 3)
    busy_level = jax.random.randint(busy_key, (array_shape[0],), 0, upper_count // 2 + 1)
    base_count = jax.random.randint(base_key, (cell_count,), 1, upper_count // 2 + 1)
    per_cell = jnp.repeat(busy_level, cell_count // array_shape[0])
    counts = jnp.minimum(upper_count, base_count + per_cell)
    spot = jax.random.randint(spot_key, (), 0, cell_count)
    positions = jnp.arange(cell_count, dtype=jnp.int32)
    counts = jnp.where(positions == spot, upper_count, counts)
    counts = jnp.where(positions == (spot + 1) % cell_count, 1, counts)
    return counts.reshape(array_shape).astype(jnp.int32)


def rating_blocks(key, array_shape, density, lowest, spread, power):
    value_key, mask_key = jax.random.split(key)
    uniform_part = jax.random.uniform(value_key, array_shape, jnp.float32)
    values = lowest + spread * uniform_part ** power
    observed = jax.random.bernoulli(mask_key, density, array_shape)
    return jnp.where(observed, values, jnp.float32(0.0)).astype(jnp.bfloat16)


def draw_user_pairs(key, part):
    key = jax.random.fold_in(key, 1)
    chosen = pick_pairs(key, DEVICES * N_BLK, CAP, UD // B * (ID // B))
    return chosen.reshape(DEVICES, N_BLK, CAP)


def draw_item_pairs(key, part):
    key = jax.random.fold_in(key, 2)
    return pick_pairs(key, DEVICES, ICAP, UD // B * (ID // B))


def draw_user_counts(key, part):
    key = jax.random.fold_in(key, 3)
    return pick_counts(key, (DEVICES, N_BLK), CAP)


def draw_live_item_counts(key, part):
    key = jax.random.fold_in(key, 4)
    return pick_counts(key, (DEVICES,), ICAP)


def draw_user_ratings(key, part):
    key = jax.random.fold_in(key, 5)
    return rating_blocks(key, (DEVICES, N_BLK, CAP, B, B), 0.5, 1.0, 4.0, 1.0)


def draw_item_ratings(key, part):
    key = jax.random.fold_in(key, 6)
    return rating_blocks(key, (DEVICES, ICAP, B, B), 0.5, 1.0, 4.0, 1.0)


def block_scale(key, extent, pieces, low, top_value):
    loudness, own = 1.0, jax.random.fold_in(key, 6)
    for position, parts in pieces:
        heights = jnp.exp(jax.random.uniform(jax.random.fold_in(own, position), (parts,), jnp.float32, low / len(pieces), top_value / len(pieces)))
        loudness = loudness * jnp.repeat(heights, extent[position] // parts).reshape([-1 if axis == position else 1 for axis in range(len(extent))])
    return loudness


def bell_draw(stream_key, dims, scale, bound, cuts=(), kind=jnp.bfloat16):
    result = jax.random.normal(stream_key, dims, jnp.float32) * scale
    if len(cuts) > 0:
        result = block_scale(stream_key, dims, cuts, -0.22, 0.18) * result
    return jnp.clip(result, min=-bound, max=bound).astype(kind)


def setup_inputs(seed: int = 0) -> dict:
    arg_keys = jax.random.split(jax.random.key(seed), 9)
    users = bell_draw(arg_keys[0], (NUSERS, R), 0.25, 1.5, ((0, 256),))
    items = bell_draw(arg_keys[1], (NITEMS, R), 0.25, 1.5, ((0, 256),))
    user_pairs = draw_user_pairs(jax.random.fold_in(arg_keys[8], 71), 0)
    user_ratings = draw_user_ratings(jax.random.fold_in(arg_keys[8], 71), 0)
    user_counts = draw_user_counts(jax.random.fold_in(arg_keys[8], 71), 0)
    item_pairs = draw_item_pairs(jax.random.fold_in(arg_keys[8], 71), 0)
    item_ratings = draw_item_ratings(jax.random.fold_in(arg_keys[8], 71), 0)
    live_item_counts = draw_live_item_counts(jax.random.fold_in(arg_keys[8], 71), 0)
    return {"users": users, "items": items, "user_pairs": user_pairs, "user_ratings": user_ratings, "user_counts": user_counts, "item_pairs": item_pairs, "item_ratings": item_ratings, "live_item_counts": live_item_counts}


user_rate = 0.03
item_rate = 0.005
shrink = 0.05


def block_loss_terms(row_factor_matrix, column_factor_matrix, ratings, slot_live):
    predicted_rating = jnp.einsum('tgo,tco->tgc', row_factor_matrix.astype(jnp.float32), column_factor_matrix.astype(jnp.float32))
    observed = (ratings != 0) & slot_live[:, None, None]
    rating_error = jnp.where(observed, ratings.astype(jnp.float32) - predicted_rating, jnp.float32(0.0)).astype(jnp.bfloat16)
    return jnp.einsum('yvg,ygt->yvt', rating_error.astype(jnp.float32), column_factor_matrix.astype(jnp.float32))


def collect(terms, block_index, count_of_blocks):
    return jax.ops.segment_sum(terms, block_index, num_segments=count_of_blocks)


def reference(users, items, user_pairs, user_ratings, user_counts, item_pairs, item_ratings, live_item_counts):
    user_blocks = UD // B
    item_rating_blocks = ID // B
    user_groups = users.reshape(DEVICES, user_blocks, B, R)
    item_groups = items.reshape(N_BLK, N_WIDE, item_rating_blocks, B, R)
    slot_source = jnp.repeat(jnp.arange(N_BLK, dtype=jnp.int32), CAP)

    def user_group(member):
        inner_index = member % N_WIDE
        own_users = user_groups[member]
        column_items = lax.dynamic_index_in_dim(item_groups, inner_index, 1, keepdims=False)
        slot_pairs = user_pairs[member].reshape(N_BLK * CAP)
        user_index = slot_pairs // item_rating_blocks
        item_index = slot_pairs % item_rating_blocks
        column_factor_matrix = column_items[slot_source, item_index]
        row_factor_matrix = own_users[user_index]
        slot_live = (jnp.arange(CAP, dtype=jnp.int32)[None, :] < user_counts[member][:, None]).reshape(N_BLK * CAP)
        terms = block_loss_terms(row_factor_matrix, column_factor_matrix, user_ratings[member].reshape(N_BLK * CAP, B, B), slot_live)
        user_total = collect(terms, user_index, user_blocks)
        old_users = own_users.astype(jnp.float32)
        return (old_users + user_rate * (user_total - shrink * old_users)).astype(jnp.bfloat16)

    new_blocks = lax.map(user_group, jnp.arange(DEVICES, dtype=jnp.int32))
    new_users = new_blocks.reshape(DEVICES * UD, R)
    relaid = new_users.reshape(N_BLK, N_WIDE, N_WIDE, UD // N_WIDE, R).transpose(0, 2, 1, 3, 4).reshape(DEVICES, user_blocks, B, R)
    item_own = items.reshape(DEVICES, item_rating_blocks, B, R)

    def item_group(member):
        slot_pairs = item_pairs[member]
        item_index = slot_pairs // user_blocks
        user_index = slot_pairs % user_blocks
        own_items = item_own[member]
        row_factor_matrix = own_items[item_index]
        column_factor_matrix = relaid[member][user_index]
        slot_live = jnp.arange(ICAP, dtype=jnp.int32) < live_item_counts[member]
        terms = block_loss_terms(row_factor_matrix, column_factor_matrix, item_ratings[member], slot_live)
        item_total = collect(terms, item_index, item_rating_blocks)
        old_items = own_items.astype(jnp.float32)
        return (old_items + item_rate * (item_total - shrink * old_items)).astype(jnp.bfloat16)

    new_items = lax.map(item_group, jnp.arange(DEVICES, dtype=jnp.int32)).reshape(DEVICES * ID, R)
    return (new_users, new_items)
```

```python
import jax
import jax.numpy as jnp
from jax import lax
from jax.experimental import pallas as pl
from jax.experimental.pallas import tpu as pltpu
from jax.sharding import PartitionSpec as P

MESH = pl.DeviceIdType.MESH

user_rate = 0.03
item_rate = 0.005
shrink = 0.05

B = 128
R = 256
UB = 32
IB = 4
NS = 8
CAP = 16
NSLOT = NS * CAP

ORDER = ((0, 0), (0, 1), (0, 3), (1, 0), (0, 2), (1, 1), (1, 3), (1, 2))


def nt(a, b):
    return lax.dot_general(a, b, (((1,), (1,)), ((), ())), preferred_element_type=jnp.float32)


def nn(a, b):
    return lax.dot_general(a, b, (((1,), (0,)), ((), ())), preferred_element_type=jnp.float32)


def kernel(
    users, items, pairs, ratings, counts, ipairs, iratings, icount,
    new_users, new_items,
    h00, h01, h02, h03, h10, h11, h12, h13,
    users_v, ur_v, ir_v, terms, nu_v, recv, acc, ni_v,
    pairs_s, counts_s, icount_s, pairs_v, ipairs_v, tab_v, tab_s,
    lsem, ursem, gs, gr, ss, rs, osem,
):
    blk = lax.axis_index("blk")
    wide = lax.axis_index("wide")
    xh, y = lax.div(blk, 4), lax.rem(blk, 4)
    xl, z, core = lax.div(wide, 16), lax.rem(lax.div(wide, 2), 8), lax.rem(wide, 2)
    held = {(0, 0): h00, (0, 1): h01, (0, 2): h02, (0, 3): h03,
            (1, 0): h10, (1, 1): h11, (1, 2): h12, (1, 3): h13}

    def slice_of(fx, dy):
        return lax.rem(xh + fx, 2) * 4 + lax.rem(y + 4 - dy, 4)

    up = (xh * 4 + lax.rem(y + 1, 4), wide)
    down = (xh * 4 + lax.rem(y + 3, 4), wide)
    across = (lax.rem(blk + 4, 8), wide)

    def partner(t, sign):
        d = lax.div(t, 4)
        dz = jnp.where(lax.rem(d, 2) == 0, lax.div(d, 2) + 1, 8 - 1 - lax.div(d, 2))
        dz = jnp.where(t >= 28, 0, dz)
        e = jnp.where(t >= 28, t - 27, lax.rem(t, 4))
        zz = lax.rem(z + 8 + sign * dz, 8)
        xx = lax.rem(xl + lax.div(e, 2), 2)
        cc = lax.rem(core + lax.rem(e, 2), 2)
        return xx * 16 + zz * 2 + cc

    barrier = pltpu.get_barrier_semaphore()
    for dev in (up, down, across):
        pl.semaphore_signal(barrier, inc=1, device_id=dev, device_id_type=MESH)

    def greet(t, carry):
        pl.semaphore_signal(barrier, inc=1, device_id=(blk, partner(t, 1)), device_id_type=MESH)
        return carry

    lax.fori_loop(0, UB - 1, greet, 0)

    local = [
        pltpu.make_async_copy(items, h00.reshape(IB * B, R), lsem.at[0]),
        pltpu.make_async_copy(pairs, pairs_v, lsem.at[1]),
        pltpu.make_async_copy(ipairs, ipairs_v, lsem.at[2]),
        pltpu.make_async_copy(pairs, pairs_s, lsem.at[3]),
        pltpu.make_async_copy(counts, counts_s, lsem.at[4]),
        pltpu.make_async_copy(icount, icount_s, lsem.at[5]),
        pltpu.make_async_copy(users, users_v.reshape(UB * B, R), lsem.at[6]),
    ]
    for copy in local:
        copy.start()
    rating_copies = []
    for j, (fx, dy) in enumerate(ORDER):
        copy = pltpu.make_async_copy(ratings.at[0, slice_of(fx, dy)], ur_v.at[j], ursem.at[j])
        copy.start()
        rating_copies.append(copy)
    irating_copy = pltpu.make_async_copy(iratings.at[0], ir_v.at[pl.ds(0, NSLOT)], lsem.at[7])
    irating_copy.start()

    pl.semaphore_wait(barrier, 3 + UB - 1)

    def send(n, src, dst, dev):
        return pltpu.make_async_remote_copy(
            src_ref=src, dst_ref=dst, send_sem=gs.at[n], recv_sem=gr.at[n], device_id=dev, device_id_type=MESH
        )

    lo, hi = pl.ds(0, IB // 2), pl.ds(IB // 2, IB // 2)
    local[0].wait()
    hops = {}

    def go(n, src, dst, dev):
        hops[n] = send(n, src, dst, dev)
        hops[n].start()

    go(0, h00, h01, up)
    go(1, h00, h03, down)
    go(2, h00, h10, across)

    terms[NSLOT] = jnp.zeros((B, R), jnp.float32)
    ir_v[NSLOT] = jnp.zeros((B, B), jnp.bfloat16)
    for n in (1, 2, 5):
        local[n].wait()
    sub = lax.broadcasted_iota(jnp.int32, (B, B), 0)
    lane = lax.broadcasted_iota(jnp.int32, (B, B), 1)
    k16 = lax.broadcasted_iota(jnp.int32, (CAP, B), 0)
    l16 = lax.broadcasted_iota(jnp.int32, (CAP, B), 1)
    spread = jnp.where(lax.rem(l16, CAP) == k16, jnp.float32(1), jnp.float32(0)).astype(jnp.bfloat16)
    wide_pairs = nn(pairs_v[0].astype(jnp.float32).astype(jnp.bfloat16), spread)
    s8 = lax.broadcasted_iota(jnp.int32, (NS, B), 0)
    j8 = lax.div(lax.broadcasted_iota(jnp.int32, (NS, B), 1), CAP)
    picked = jnp.zeros((NS, B), jnp.bool_)
    for j, (fx, dy) in enumerate(ORDER):
        picked = picked | ((j8 == j) & (s8 == slice_of(fx, dy)))
    pair_row = jnp.sum(jnp.where(picked, wide_pairs, 0.0), axis=0, keepdims=True)
    user_row = jnp.floor(pair_row * 0.25)
    user_here = jnp.broadcast_to(user_row, (B, B))
    user_there = user_here.T
    before = jnp.max(jnp.where((user_here == user_there) & (sub < lane), sub, -1), axis=0, keepdims=True)
    last = jnp.max(jnp.where(user_there == lane.astype(jnp.float32), sub, -1), axis=0, keepdims=True)
    item_row = jnp.broadcast_to(ipairs_v[...].astype(jnp.float32), (B, B)).T
    slot_of = jnp.min(
        jnp.where((item_row == lane.astype(jnp.float32)) & (sub < icount_s[0]), sub, NSLOT), axis=0, keepdims=True
    )
    tab_v[0:1, :] = jnp.where(before < 0, NSLOT, before)
    tab_v[1:2, :] = jnp.where(last < 0, NSLOT, last)
    tab_v[2:3, :] = slot_of
    tab_copy = pltpu.make_async_copy(tab_v, tab_s, lsem.at[8])
    tab_copy.start()
    for n in (3, 4, 6):
        local[n].wait()
    tab_copy.wait()

    STEP = 4

    def work(j):
        fx, dy = ORDER[j]
        cols_ref = held[(fx, dy)]
        s = slice_of(fx, dy)
        rating_copies[j].wait()
        live = counts_s[0, s]

        def body(g, carry):
            cols, errs = [], []
            for e in range(STEP):
                k = g * STEP + e
                p = pairs_s[0, s, k]
                rows = users_v[lax.shift_right_logical(p, 2)]
                col = cols_ref[lax.bitwise_and(p, 3)]
                r = ur_v[j, k].astype(jnp.float32)
                seen = (r != 0) & (k < live)
                errs.append(jnp.where(seen, r - nt(rows, col), 0.0).astype(jnp.bfloat16))
                cols.append(col)
            for e in range(STEP):
                n = j * CAP + g * STEP + e
                terms[n] = terms[tab_s[0, n]] + nn(errs[e], cols[e])
            return carry

        lax.fori_loop(0, CAP // STEP, body, 0)

    work(0)
    hops[0].wait_recv()
    go(3, h01.at[lo], h02.at[lo], up)
    hops[1].wait_recv()
    go(4, h03.at[hi], h02.at[hi], down)
    hops[2].wait_recv()
    go(5, h10, h11, up)
    go(6, h10, h13, down)
    work(1)
    work(2)
    work(3)
    hops[3].wait_recv()
    hops[4].wait_recv()
    work(4)
    hops[5].wait_recv()
    go(7, h11.at[lo], h12.at[lo], up)
    hops[6].wait_recv()
    go(8, h13.at[hi], h12.at[hi], down)
    work(5)
    work(6)
    hops[7].wait_recv()
    hops[8].wait_recv()
    work(7)

    def update(u):
        old = users_v[u].astype(jnp.float32)
        total = terms[tab_s[1, u]]
        nu_v[u] = (old + user_rate * (total - shrink * old)).astype(jnp.bfloat16)

    def relay(t):
        u = partner(t, 1)
        return pltpu.make_async_remote_copy(
            src_ref=nu_v.at[u], dst_ref=recv.at[t], send_sem=ss.at[t], recv_sem=rs.at[t],
            device_id=(blk, u), device_id_type=MESH,
        )

    def send_out(t, carry):
        update(partner(t, 1))
        relay(t).start()
        return carry

    lax.fori_loop(0, UB - 1, send_out, 0)
    update(wide)
    recv[UB - 1] = nu_v[wide]
    users_out = pltpu.make_async_copy(nu_v.reshape(UB * B, R), new_users, osem.at[0])
    users_out.start()
    irating_copy.wait()
    acc[...] = jnp.zeros_like(acc)

    def absorb(first, second, t):
        both = recv[pl.ds(t, 2)].reshape(2 * B, R)
        for i in range(IB):
            rate = jnp.concatenate(
                [ir_v[tab_s[2, i * UB + first]], ir_v[tab_s[2, i * UB + second]]], axis=1
            ).astype(jnp.float32)
            err = jnp.where(rate != 0, rate - nt(h00[i], both), 0.0).astype(jnp.bfloat16)
            acc[i] += nn(err, both)

    def take(q, carry):
        t = q * 2
        relay(t).wait_recv()
        relay(t + 1).wait_recv()
        absorb(partner(t, -1), partner(t + 1, -1), t)
        return carry

    lax.fori_loop(0, UB // 2 - 1, take, 0)
    relay(UB - 2).wait_recv()
    absorb(partner(UB - 2, -1), wide, UB - 2)
    old = h00[...].astype(jnp.float32)
    ni_v[...] = (old + item_rate * (acc[...] - shrink * old)).astype(jnp.bfloat16)
    items_out = pltpu.make_async_copy(ni_v.reshape(IB * B, R), new_items, osem.at[1])
    items_out.start()

    for n in hops:
        hops[n].wait_send()

    def sent(t, carry):
        relay(t).wait_send()
        return carry

    lax.fori_loop(0, UB - 1, sent, 0)
    users_out.wait()
    items_out.wait()


def per_device(
    users, items, user_pairs, user_ratings, user_counts, item_pairs, item_ratings, live_item_counts
):
    bf, f32, i32 = jnp.bfloat16, jnp.float32, jnp.int32
    return pl.pallas_call(
        kernel,
        out_shape=(
            jax.ShapeDtypeStruct(users.shape, bf),
            jax.ShapeDtypeStruct(items.shape, bf),
        ),
        in_specs=[pl.BlockSpec(memory_space=pl.ANY)] * 8,
        out_specs=(pl.BlockSpec(memory_space=pl.ANY), pl.BlockSpec(memory_space=pl.ANY)),
        scratch_shapes=[pltpu.VMEM((IB, B, R), bf)] * 8
        + [
            pltpu.VMEM((UB, B, R), bf),
            pltpu.VMEM((NS, CAP, B, B), bf),
            pltpu.VMEM((NSLOT + 1, B, B), bf),
            pltpu.VMEM((NSLOT + 1, B, R), f32),
            pltpu.VMEM((UB, B, R), bf),
            pltpu.VMEM((UB, B, R), bf),
            pltpu.VMEM((IB, B, R), f32),
            pltpu.VMEM((IB, B, R), bf),
            pltpu.SMEM((1, NS, CAP), i32),
            pltpu.SMEM((1, NS), i32),
            pltpu.SMEM((1,), i32),
            pltpu.VMEM((1, NS, CAP), i32),
            pltpu.VMEM((1, NSLOT), i32),
            pltpu.VMEM((8, 128), i32),
            pltpu.SMEM((8, 128), i32),
            pltpu.SemaphoreType.DMA((9,)),
            pltpu.SemaphoreType.DMA((NS,)),
            pltpu.SemaphoreType.DMA((9,)),
            pltpu.SemaphoreType.DMA((9,)),
            pltpu.SemaphoreType.DMA((UB - 1,)),
            pltpu.SemaphoreType.DMA((UB - 1,)),
            pltpu.SemaphoreType.DMA((2,)),
        ],
        compiler_params=pltpu.CompilerParams(
            collective_id=0, has_side_effects=True, vmem_limit_bytes=52 * 2**20
        ),
        name="round",
    )(users, items, user_pairs, user_ratings, user_counts, item_pairs, item_ratings, live_item_counts)


def solution(mesh):
    return jax.shard_map(
        per_device,
        mesh=mesh,
        in_specs=(
            P(("blk", "wide"), None),
            P(("blk", "wide"), None),
            P(("blk", "wide"), None, None),
            P(("blk", "wide"), None, None, None, None),
            P(("blk", "wide"), None),
            P(("blk", "wide"), None),
            P(("blk", "wide"), None, None, None),
            P(("blk", "wide")),
        ),
        out_specs=(P(("blk", "wide"), None), P(("blk", "wide"), None)),
        check_vma=False,
    )
```

```python
import jax
import jax.numpy as jnp
from jax import lax
from jax.experimental import pallas as pl
from jax.experimental.pallas import tpu as pltpu
from jax.sharding import PartitionSpec as P

MESH = pl.DeviceIdType.MESH

user_rate = 0.03
item_rate = 0.005
shrink = 0.05

B = 128
R = 256
UB = 32
IB = 4
NS = 8
CAP = 16
NSLOT = NS * CAP
VMEM = 62 * 2**20
PIECES = 4

ORDER = ((0, 0), (0, 1), (0, 3), (1, 0), (0, 2), (1, 1), (1, 3), (1, 2))


def nt(a, b):
    return lax.dot_general(a, b, (((1,), (1,)), ((), ())), preferred_element_type=jnp.float32)


def nn(a, b):
    return lax.dot_general(a, b, (((1,), (0,)), ((), ())), preferred_element_type=jnp.float32)


def kernel(
    users, items, pairs, ratings, counts, ipairs, iratings, icount,
    new_users, new_items,
    h00, h01, h02, h03, h10, h11, h12, h13,
    users_v, ur_v, ir_v, terms, nu_v, recv, acc, ni_v,
    pairs_s, counts_s, icount_s, pairs_v, ipairs_v, tab_v, tab_s,
    lsem, ursem, gs, gr, ss, rs, osem, token, entered,
):
    blk = lax.axis_index("blk")
    wide = lax.axis_index("wide")
    xh, y = lax.div(blk, 4), lax.rem(blk, 4)
    xl, z, core = lax.div(wide, 16), lax.rem(lax.div(wide, 2), 8), lax.rem(wide, 2)
    held = {(0, 0): h00, (0, 1): h01, (0, 2): h02, (0, 3): h03,
            (1, 0): h10, (1, 1): h11, (1, 2): h12, (1, 3): h13}

    def slice_of(fx, dy):
        return lax.rem(xh + fx, 2) * 4 + lax.rem(y + 4 - dy, 4)

    up = (xh * 4 + lax.rem(y + 1, 4), wide)
    down = (xh * 4 + lax.rem(y + 3, 4), wide)
    across = (lax.rem(blk + 4, 8), wide)

    def partner(t, sign):
        d = lax.div(t, 4)
        dz = jnp.where(lax.rem(d, 2) == 0, lax.div(d, 2) + 1, 8 - 1 - lax.div(d, 2))
        dz = jnp.where(t >= 28, 0, dz)
        e = jnp.where(t >= 28, t - 27, lax.rem(t, 4))
        zz = lax.rem(z + 8 + sign * dz, 8)
        xx = lax.rem(xl + lax.div(e, 2), 2)
        cc = lax.rem(core + lax.rem(e, 2), 2)
        return xx * 16 + zz * 2 + cc

    place = z
    below = xl * 16 + lax.rem(z + 7, 8) * 2 + core
    above = xl * 16 + lax.rem(z + 1, 8) * 2 + core
    plane = (
        xl * 16 + z * 2 + 1 - core,
        (1 - xl) * 16 + z * 2 + core,
        (1 - xl) * 16 + z * 2 + 1 - core,
    )
    barrier = pltpu.get_barrier_semaphore()
    for dev in (up, down, across):
        pl.semaphore_signal(barrier, inc=1, device_id=dev, device_id_type=MESH)
    for dev in plane:
        pl.semaphore_signal(barrier, inc=1, device_id=(blk, dev), device_id_type=MESH)

    @pl.when(place > 0)
    def _():
        pl.semaphore_signal(barrier, inc=1, device_id=(blk, below), device_id_type=MESH)

    local = [
        pltpu.make_async_copy(items, h00, lsem.at[0]),
        pltpu.make_async_copy(pairs, pairs_v, lsem.at[1]),
        pltpu.make_async_copy(ipairs, ipairs_v, lsem.at[2]),
        pltpu.make_async_copy(pairs, pairs_s, lsem.at[3]),
        pltpu.make_async_copy(counts, counts_s, lsem.at[4]),
        pltpu.make_async_copy(icount, icount_s, lsem.at[5]),
        pltpu.make_async_copy(users, users_v, lsem.at[6]),
    ]
    for copy in local:
        copy.start()
    rating_copies = []
    for j, (fx, dy) in enumerate(ORDER):
        copy = pltpu.make_async_copy(ratings.at[0, slice_of(fx, dy)], ur_v.at[j], ursem.at[j])
        copy.start()
        rating_copies.append(copy)
    irating_copy = pltpu.make_async_copy(iratings.at[0], ir_v.at[pl.ds(0, NSLOT)], lsem.at[7])
    irating_copy.start()

    pl.semaphore_wait(barrier, 6 + jnp.where(place < 7, 1, 0))

    def send(n, src, dst, dev):
        return pltpu.make_async_remote_copy(
            src_ref=src, dst_ref=dst, send_sem=gs.at[n], recv_sem=gr.at[n], device_id=dev, device_id_type=MESH
        )

    lo, hi = pl.ds(0, IB // 2), pl.ds(IB // 2, IB // 2)
    hops = {}

    def go(n, src, dst, half, dev):
        hops[n] = send(n, src.at[half], dst.at[half], dev)
        hops[n].start()

    go(0, items, h01, lo, up)
    go(1, items, h03, hi, down)
    go(2, items, h10, lo, across)
    go(3, items, h10, hi, across)
    go(4, items, h01, hi, up)
    go(5, items, h03, lo, down)

    @pl.when(place > 0)
    def _():
        pl.semaphore_wait(token, 1)

    @pl.when(place < 7)
    def _():
        pl.semaphore_signal(token, inc=1, device_id=(blk, above), device_id_type=MESH)

    def greet(n, carry):
        e, zz = lax.rem(n, 4), lax.div(n, 4)
        dev = lax.div(e, 2) * 16 + zz * 2 + lax.rem(e, 2)
        pl.semaphore_signal(entered, inc=1, device_id=(blk, dev), device_id_type=MESH)
        return carry

    lax.fori_loop(0, 4 * place, greet, 0)

    terms[NSLOT] = jnp.zeros((B, R), jnp.float32)
    ir_v[NSLOT] = jnp.zeros((B, B), jnp.bfloat16)
    for n in (1, 2, 5):
        local[n].wait()
    sub = lax.broadcasted_iota(jnp.int32, (B, B), 0)
    lane = lax.broadcasted_iota(jnp.int32, (B, B), 1)
    k16 = lax.broadcasted_iota(jnp.int32, (CAP, B), 0)
    l16 = lax.broadcasted_iota(jnp.int32, (CAP, B), 1)
    spread = jnp.where(lax.rem(l16, CAP) == k16, jnp.float32(1), jnp.float32(0)).astype(jnp.bfloat16)
    wide_pairs = nn(pairs_v[0].astype(jnp.float32).astype(jnp.bfloat16), spread)
    s8 = lax.broadcasted_iota(jnp.int32, (NS, B), 0)
    j8 = lax.div(lax.broadcasted_iota(jnp.int32, (NS, B), 1), CAP)
    picked = jnp.zeros((NS, B), jnp.bool_)
    for j, (fx, dy) in enumerate(ORDER):
        picked = picked | ((j8 == j) & (s8 == slice_of(fx, dy)))
    pair_row = jnp.sum(jnp.where(picked, wide_pairs, 0.0), axis=0, keepdims=True)
    user_row = jnp.floor(pair_row * 0.25)
    user_here = jnp.broadcast_to(user_row, (B, B))
    user_there = user_here.T
    before = jnp.max(jnp.where((user_here == user_there) & (sub < lane), sub, -1), axis=0, keepdims=True)
    last = jnp.max(jnp.where(user_there == lane.astype(jnp.float32), sub, -1), axis=0, keepdims=True)
    item_row = jnp.broadcast_to(ipairs_v[...].astype(jnp.float32), (B, B)).T
    slot_of = jnp.min(
        jnp.where((item_row == lane.astype(jnp.float32)) & (sub < icount_s[0]), sub, NSLOT), axis=0, keepdims=True
    )
    tab_v[0:1, :] = jnp.where(before < 0, NSLOT, before)
    tab_v[1:2, :] = jnp.where(last < 0, NSLOT, last)
    tab_v[2:3, :] = slot_of
    tab_copy = pltpu.make_async_copy(tab_v, tab_s, lsem.at[8])
    tab_copy.start()
    for n in (3, 4, 6):
        local[n].wait()
    tab_copy.wait()

    STEP = 8

    def work(j):
        fx, dy = ORDER[j]
        cols_ref = held[(fx, dy)]
        s = slice_of(fx, dy)
        rating_copies[j].wait()
        live = counts_s[0, s]

        def body(g, carry):
            cols, errs = [], []
            for e in range(STEP):
                k = g * STEP + e
                p = pairs_s[0, s, k]
                rows = users_v[lax.shift_right_logical(p, 2)]
                col = cols_ref[lax.bitwise_and(p, 3)]
                r = ur_v[j, k].astype(jnp.float32)
                seen = (r != 0) & (k < live)
                errs.append(jnp.where(seen, r - nt(rows, col), 0.0).astype(jnp.bfloat16))
                cols.append(col)
            for e in range(STEP):
                n = j * CAP + g * STEP + e
                terms[n] = terms[tab_s[0, n]] + nn(errs[e], cols[e])
            return carry

        lax.fori_loop(0, CAP // STEP, body, 0)

    local[0].wait()
    work(0)
    hops[0].wait_recv()
    go(6, h01, h02, lo, up)
    go(7, h01, h11, lo, across)
    hops[1].wait_recv()
    go(8, h03, h02, hi, down)
    go(9, h03, h13, hi, across)
    hops[2].wait_recv()
    hops[3].wait_recv()
    go(10, h10, h11, hi, up)
    go(11, h10, h13, lo, down)
    hops[4].wait_recv()
    work(1)
    hops[5].wait_recv()
    work(2)
    work(3)
    hops[6].wait_recv()
    hops[8].wait_recv()
    work(4)
    hops[7].wait_recv()
    go(12, h11, h12, lo, up)
    hops[9].wait_recv()
    go(13, h13, h12, hi, down)
    hops[10].wait_recv()
    work(5)
    hops[11].wait_recv()
    work(6)
    hops[12].wait_recv()
    hops[13].wait_recv()
    work(7)

    @pl.when(place < 7)
    def _():
        pl.semaphore_wait(entered, 4 * (7 - place))

    def update(u):
        old = users_v[u].astype(jnp.float32)
        total = terms[tab_s[1, u]]
        nu_v[u] = (old + user_rate * (total - shrink * old)).astype(jnp.bfloat16)

    def relay(t):
        u = partner(t, 1)
        return pltpu.make_async_remote_copy(
            src_ref=nu_v.at[u], dst_ref=recv.at[t], send_sem=ss.at[t], recv_sem=rs.at[t],
            device_id=(blk, u), device_id_type=MESH,
        )

    def send_out(t, carry):
        update(partner(t, 1))
        relay(t).start()
        return carry

    lax.fori_loop(0, UB - 1, send_out, 0)
    update(wide)
    recv[UB - 1] = nu_v[wide]
    users_out = pltpu.make_async_copy(nu_v, new_users, osem.at[0])
    users_out.start()
    irating_copy.wait()
    acc[...] = jnp.zeros_like(acc)

    GROUP = 4

    def absorb(t, owners):
        some = recv[pl.ds(t, GROUP)].reshape(GROUP * B, R)
        guess = nt(h00[...].reshape(IB * B, R), some)
        errs = []
        for i in range(IB):
            rate = jnp.concatenate([ir_v[tab_s[2, i * UB + u]] for u in owners], axis=1).astype(jnp.float32)
            errs.append(jnp.where(rate != 0, rate - guess[i * B : (i + 1) * B], 0.0).astype(jnp.bfloat16))
        acc[...] += nn(jnp.concatenate(errs, axis=0), some).reshape(IB, B, R)

    def take(q, carry):
        t = q * GROUP
        for e in range(GROUP):
            relay(t + e).wait_recv()
        absorb(t, [partner(t + e, -1) for e in range(GROUP)])
        return carry

    lax.fori_loop(0, UB // GROUP - 1, take, 0)
    t = UB - GROUP
    for e in range(GROUP - 1):
        relay(t + e).wait_recv()
    absorb(t, [partner(t + e, -1) for e in range(GROUP - 1)] + [wide])
    old = h00[...].astype(jnp.float32)
    ni_v[...] = (old + item_rate * (acc[...] - shrink * old)).astype(jnp.bfloat16)
    items_out = pltpu.make_async_copy(ni_v, new_items, osem.at[1])
    items_out.start()

    for n in hops:
        hops[n].wait_send()

    def sent(t, carry):
        relay(t).wait_send()
        return carry

    lax.fori_loop(0, UB - 1, sent, 0)
    users_out.wait()
    items_out.wait()


def deliver(made_users, made_items, new_users, new_items, held_users, held_items, insem, outsem):
    parts = [(made_items, held_items, new_items)]
    for n in range(PIECES):
        part = pl.ds(n * (UB // PIECES), UB // PIECES)
        parts.append((made_users.at[part], held_users.at[part], new_users.at[part]))
    reads = [pltpu.make_async_copy(a, b, insem.at[n]) for n, (a, b, c) in enumerate(parts)]
    writes = [pltpu.make_async_copy(b, c, outsem.at[n]) for n, (a, b, c) in enumerate(parts)]
    for copy in reads:
        copy.start()
    for read, write in zip(reads, writes):
        read.wait()
        write.start()
    for copy in writes:
        copy.wait()


def per_device(
    users, items, user_pairs, user_ratings, user_counts, item_pairs, item_ratings, live_item_counts
):
    bf, f32, i32 = jnp.bfloat16, jnp.float32, jnp.int32
    made_users, made_items = pl.pallas_call(
        kernel,
        out_shape=(
            jax.ShapeDtypeStruct((UB, B, R), bf),
            jax.ShapeDtypeStruct((IB, B, R), bf),
        ),
        in_specs=[pl.BlockSpec(memory_space=pl.ANY)] * 8,
        out_specs=(pl.BlockSpec(memory_space=pl.ANY), pl.BlockSpec(memory_space=pl.ANY)),
        scratch_shapes=[pltpu.VMEM((IB, B, R), bf)] * 8
        + [
            pltpu.VMEM((UB, B, R), bf),
            pltpu.VMEM((NS, CAP, B, B), bf),
            pltpu.VMEM((NSLOT + 1, B, B), bf),
            pltpu.VMEM((NSLOT + 1, B, R), f32),
            pltpu.VMEM((UB, B, R), bf),
            pltpu.VMEM((UB, B, R), bf),
            pltpu.VMEM((IB, B, R), f32),
            pltpu.VMEM((IB, B, R), bf),
            pltpu.SMEM((1, NS, CAP), i32),
            pltpu.SMEM((1, NS), i32),
            pltpu.SMEM((1,), i32),
            pltpu.VMEM((1, NS, CAP), i32),
            pltpu.VMEM((1, NSLOT), i32),
            pltpu.VMEM((8, 128), i32),
            pltpu.SMEM((8, 128), i32),
            pltpu.SemaphoreType.DMA((9,)),
            pltpu.SemaphoreType.DMA((NS,)),
            pltpu.SemaphoreType.DMA((14,)),
            pltpu.SemaphoreType.DMA((14,)),
            pltpu.SemaphoreType.DMA((UB - 1,)),
            pltpu.SemaphoreType.DMA((UB - 1,)),
            pltpu.SemaphoreType.DMA((2,)),
            pltpu.SemaphoreType.REGULAR,
            pltpu.SemaphoreType.REGULAR,
        ],
        compiler_params=pltpu.CompilerParams(
            collective_id=0, has_side_effects=True, vmem_limit_bytes=VMEM
        ),
        name="round",
    )(
        users.reshape(UB, B, R), items.reshape(IB, B, R),
        user_pairs, user_ratings, user_counts, item_pairs, item_ratings, live_item_counts,
    )
    new_users, new_items = pl.pallas_call(
        deliver,
        out_shape=(
            jax.ShapeDtypeStruct((UB, B, R), bf),
            jax.ShapeDtypeStruct((IB, B, R), bf),
        ),
        in_specs=[pl.BlockSpec(memory_space=pl.ANY)] * 2,
        out_specs=(pl.BlockSpec(memory_space=pl.ANY), pl.BlockSpec(memory_space=pl.ANY)),
        scratch_shapes=[
            pltpu.VMEM((UB, B, R), bf),
            pltpu.VMEM((IB, B, R), bf),
            pltpu.SemaphoreType.DMA((PIECES + 1,)),
            pltpu.SemaphoreType.DMA((PIECES + 1,)),
        ],
        compiler_params=pltpu.CompilerParams(vmem_limit_bytes=VMEM),
        name="deliver",
    )(made_users, made_items)
    return new_users.reshape(users.shape), new_items.reshape(items.shape)


def solution(mesh):
    return jax.shard_map(
        per_device,
        mesh=mesh,
        in_specs=(
            P(("blk", "wide"), None),
            P(("blk", "wide"), None),
            P(("blk", "wide"), None, None),
            P(("blk", "wide"), None, None, None, None),
            P(("blk", "wide"), None),
            P(("blk", "wide"), None),
            P(("blk", "wide"), None, None, None),
            P(("blk", "wide")),
        ),
        out_specs=(P(("blk", "wide"), None), P(("blk", "wide"), None)),
        check_vma=False,
    )
```

```python
import jax
import jax.numpy as jnp
from jax import lax
from jax.experimental import pallas as pl
from jax.experimental.pallas import tpu as pltpu
from jax.sharding import PartitionSpec as P

MESH = pl.DeviceIdType.MESH

user_rate = 0.03
item_rate = 0.005
shrink = 0.05

B = 128
R = 256
UB = 32
IB = 4
NS = 8
CAP = 16
NSLOT = NS * CAP
VMEM = 61 * 2**20
GROUP = 4
EARLY = 2
SENDS = ((4, 3, 5, 2, 6, 1, 7), (4, 3, 5, 2, 6, 1, 7))
TAKES = ((4, 3, 5, 2, 6, 1, 7), (4, 3, 5, 2, 6, 1, 7))

ORDER = ((0, 0), (0, 1), (0, 3), (1, 0), (0, 2), (1, 1), (1, 3), (1, 2))


def nt(a, b):
    return lax.dot_general(a, b, (((1,), (1,)), ((), ())), preferred_element_type=jnp.float32)


def nn(a, b):
    return lax.dot_general(a, b, (((1,), (0,)), ((), ())), preferred_element_type=jnp.float32)


def kernel(
    users, items, pairs, ratings, counts, ipairs, iratings, icount,
    nu_v, ni_v,
    h00, h01, h02, h03, h10, h11, h12, h13,
    users_v, ur_v, ir_v, terms, recv, acc,
    pairs_s, counts_s, icount_s, pairs_v, ipairs_v, tab_v, tab_s,
    lsem, ursem, gs, gr, ss, rs, token, entered,
):
    blk = lax.axis_index("blk")
    wide = lax.axis_index("wide")
    xh, y = lax.div(blk, 4), lax.rem(blk, 4)
    xl, z, core = lax.div(wide, 16), lax.rem(lax.div(wide, 2), 8), lax.rem(wide, 2)
    held = {(0, 0): h00, (0, 1): h01, (0, 2): h02, (0, 3): h03,
            (1, 0): h10, (1, 1): h11, (1, 2): h12, (1, 3): h13}

    def slice_of(fx, dy):
        return lax.rem(xh + fx, 2) * 4 + lax.rem(y + 4 - dy, 4)

    up = (xh * 4 + lax.rem(y + 1, 4), wide)
    down = (xh * 4 + lax.rem(y + 3, 4), wide)
    across = (lax.rem(blk + 4, 8), wide)

    def partner(t, sign):
        dz = lax.rem(lax.div(t, 4) + 1, 8)
        e = lax.rem(t, 4)
        xx = lax.rem(xl + lax.div(e, 2), 2)
        cc = lax.rem(core + lax.rem(e, 2), 2)
        zz = lax.rem(z + 8 + sign * dz, 8)
        return xx * 16 + zz * 2 + cc

    def slot(n, order):
        dz = 0
        for m in range(7):
            dz = jnp.where(n == m, jnp.where(z < 4, order[0][m], order[1][m]), dz)
        return (dz - 1) * 4

    place = z
    below = xl * 16 + lax.rem(z + 7, 8) * 2 + core
    above = xl * 16 + lax.rem(z + 1, 8) * 2 + core
    plane = (
        xl * 16 + z * 2 + 1 - core,
        (1 - xl) * 16 + z * 2 + core,
        (1 - xl) * 16 + z * 2 + 1 - core,
    )
    barrier = pltpu.get_barrier_semaphore()
    for dev in (up, down, across):
        pl.semaphore_signal(barrier, inc=1, device_id=dev, device_id_type=MESH)
    for dev in plane:
        pl.semaphore_signal(barrier, inc=1, device_id=(blk, dev), device_id_type=MESH)

    @pl.when(place > 0)
    def _():
        pl.semaphore_signal(barrier, inc=1, device_id=(blk, below), device_id_type=MESH)

    local = [
        pltpu.make_async_copy(items, h00, lsem.at[0]),
        pltpu.make_async_copy(pairs, pairs_v, lsem.at[1]),
        pltpu.make_async_copy(ipairs, ipairs_v, lsem.at[2]),
        pltpu.make_async_copy(pairs, pairs_s, lsem.at[3]),
        pltpu.make_async_copy(counts, counts_s, lsem.at[4]),
        pltpu.make_async_copy(icount, icount_s, lsem.at[5]),
        pltpu.make_async_copy(users, users_v, lsem.at[6]),
    ]
    for copy in local:
        copy.start()
    rating_copies = [
        pltpu.make_async_copy(ratings.at[0, slice_of(fx, dy)], ur_v.at[j], ursem.at[j])
        for j, (fx, dy) in enumerate(ORDER)
    ]
    rating_copies[0].start()
    irating_copy = pltpu.make_async_copy(iratings.at[0], ir_v.at[pl.ds(0, NSLOT)], lsem.at[7])

    pl.semaphore_wait(barrier, 6 + jnp.where(place < 7, 1, 0))

    def send(n, src, dst, dev):
        return pltpu.make_async_remote_copy(
            src_ref=src, dst_ref=dst, send_sem=gs.at[n], recv_sem=gr.at[n], device_id=dev, device_id_type=MESH
        )

    lo, hi = pl.ds(0, IB // 2), pl.ds(IB // 2, IB // 2)
    hops = {}

    def go(n, src, dst, half, dev):
        hops[n] = send(n, src.at[half], dst.at[half], dev)
        hops[n].start()

    go(0, items, h01, lo, up)
    go(1, items, h03, hi, down)
    go(2, items, h10, lo, across)
    go(3, items, h10, hi, across)
    go(4, items, h01, hi, up)
    go(5, items, h03, lo, down)
    for copy in rating_copies[1:]:
        copy.start()

    @pl.when(place > 0)
    def _():
        pl.semaphore_wait(token, 1)

    @pl.when(place < 7)
    def _():
        pl.semaphore_signal(token, inc=1, device_id=(blk, above), device_id_type=MESH)

    def greet(n, carry):
        e, zz = lax.rem(n, 4), lax.div(n, 4)
        dev = lax.div(e, 2) * 16 + zz * 2 + lax.rem(e, 2)
        pl.semaphore_signal(entered, inc=1, device_id=(blk, dev), device_id_type=MESH)
        return carry

    lax.fori_loop(0, 4 * place, greet, 0)

    terms[NSLOT] = jnp.zeros((B, R), jnp.float32)
    ir_v[NSLOT] = jnp.zeros((B, B), jnp.bfloat16)
    for n in (1, 2, 5):
        local[n].wait()
    sub = lax.broadcasted_iota(jnp.int32, (B, B), 0)
    lane = lax.broadcasted_iota(jnp.int32, (B, B), 1)
    k16 = lax.broadcasted_iota(jnp.int32, (CAP, B), 0)
    l16 = lax.broadcasted_iota(jnp.int32, (CAP, B), 1)
    spread = jnp.where(lax.rem(l16, CAP) == k16, jnp.float32(1), jnp.float32(0)).astype(jnp.bfloat16)
    wide_pairs = nn(pairs_v[0].astype(jnp.float32).astype(jnp.bfloat16), spread)
    s8 = lax.broadcasted_iota(jnp.int32, (NS, B), 0)
    j8 = lax.div(lax.broadcasted_iota(jnp.int32, (NS, B), 1), CAP)
    picked = jnp.zeros((NS, B), jnp.bool_)
    for j, (fx, dy) in enumerate(ORDER):
        picked = picked | ((j8 == j) & (s8 == slice_of(fx, dy)))
    pair_row = jnp.sum(jnp.where(picked, wide_pairs, 0.0), axis=0, keepdims=True)
    user_row = jnp.floor(pair_row * 0.25)
    user_here = jnp.broadcast_to(user_row, (B, B))
    user_there = user_here.T
    before = jnp.max(jnp.where((user_here == user_there) & (sub < lane), sub, -1), axis=0, keepdims=True)
    last = jnp.max(jnp.where(user_there == lane.astype(jnp.float32), sub, -1), axis=0, keepdims=True)
    item_row = jnp.broadcast_to(ipairs_v[...].astype(jnp.float32), (B, B)).T
    slot_of = jnp.min(
        jnp.where((item_row == lane.astype(jnp.float32)) & (sub < icount_s[0]), sub, NSLOT), axis=0, keepdims=True
    )
    tab_v[0:1, :] = jnp.where(before < 0, NSLOT, before)
    tab_v[1:2, :] = jnp.where(last < 0, NSLOT, last)
    tab_v[2:3, :] = slot_of
    tab_copy = pltpu.make_async_copy(tab_v, tab_s, lsem.at[8])
    tab_copy.start()
    for n in (3, 4, 6):
        local[n].wait()
    tab_copy.wait()

    def work(j):
        STEP = CAP if j == NS - 1 else 8
        fx, dy = ORDER[j]
        cols_ref = held[(fx, dy)]
        s = slice_of(fx, dy)
        rating_copies[j].wait()
        live = counts_s[0, s]

        def body(g, carry):
            cols, errs = [], []
            for e in range(STEP):
                k = g * STEP + e
                p = pairs_s[0, s, k]
                rows = users_v[lax.shift_right_logical(p, 2)]
                col = cols_ref[lax.bitwise_and(p, 3)]
                r = ur_v[j, k].astype(jnp.float32)
                seen = (r != 0) & (k < live)
                errs.append(jnp.where(seen, r - nt(rows, col), 0.0).astype(jnp.bfloat16))
                cols.append(col)
            for e in range(STEP):
                n = j * CAP + g * STEP + e
                terms[n] = terms[tab_s[0, n]] + nn(errs[e], cols[e])
            return carry

        lax.fori_loop(0, CAP // STEP, body, 0)

    local[0].wait()
    work(0)
    hops[0].wait_recv()
    go(6, h01, h02, lo, up)
    go(7, h01, h11, lo, across)
    hops[1].wait_recv()
    go(8, h03, h02, hi, down)
    go(9, h03, h13, hi, across)
    hops[2].wait_recv()
    hops[3].wait_recv()
    go(10, h10, h11, hi, up)
    go(11, h10, h13, lo, down)
    hops[4].wait_recv()
    work(1)
    hops[5].wait_recv()
    work(2)
    work(3)
    irating_copy.start()
    hops[6].wait_recv()
    hops[8].wait_recv()
    work(4)
    hops[7].wait_recv()
    go(12, h11, h12, lo, up)
    hops[9].wait_recv()
    go(13, h13, h12, hi, down)
    hops[10].wait_recv()
    work(5)
    hops[11].wait_recv()
    work(6)
    hops[12].wait_recv()
    hops[13].wait_recv()
    work(7)

    @pl.when(place < 7)
    def _():
        pl.semaphore_wait(entered, 4 * (7 - place))

    def update(u):
        old = users_v[u].astype(jnp.float32)
        total = terms[tab_s[1, u]]
        nu_v[u] = (old + user_rate * (total - shrink * old)).astype(jnp.bfloat16)

    def relay(t):
        u = partner(t, 1)
        return pltpu.make_async_remote_copy(
            src_ref=nu_v.at[u], dst_ref=recv.at[t], send_sem=ss.at[t], recv_sem=rs.at[t],
            device_id=(blk, u), device_id_type=MESH,
        )

    def send_out(n, carry):
        first = slot(n, SENDS)
        for e in range(GROUP):
            update(partner(first + e, 1))
            relay(first + e).start()
        return carry

    lax.fori_loop(0, EARLY, send_out, 0)
    for t in range(UB - GROUP + 1, UB):
        update(partner(t, 1))
        relay(t).start()
    lax.fori_loop(EARLY, UB // GROUP - 1, send_out, 0)
    update(wide)
    recv[UB - GROUP] = nu_v[wide]
    irating_copy.wait()
    acc[...] = jnp.zeros_like(acc)

    def absorb(t, owners):
        some = recv[pl.ds(t, GROUP)].reshape(GROUP * B, R)
        guess = nt(h00[...].reshape(IB * B, R), some)
        errs = []
        for i in range(IB):
            rate = jnp.concatenate([ir_v[tab_s[2, i * UB + u]] for u in owners], axis=1).astype(jnp.float32)
            errs.append(jnp.where(rate != 0, rate - guess[i * B : (i + 1) * B], 0.0).astype(jnp.bfloat16))
        acc[...] += nn(jnp.concatenate(errs, axis=0), some).reshape(IB, B, R)

    def take(n, carry):
        t = slot(n, TAKES)
        for e in range(GROUP):
            relay(t + e).wait_recv()
        absorb(t, [partner(t + e, -1) for e in range(GROUP)])
        return carry

    lax.fori_loop(0, EARLY, take, 0)
    t = UB - GROUP
    for e in range(1, GROUP):
        relay(t + e).wait_recv()
    absorb(t, [wide] + [partner(t + e, -1) for e in range(1, GROUP)])
    lax.fori_loop(EARLY, UB // GROUP - 1, take, 0)
    old = h00[...].astype(jnp.float32)
    ni_v[...] = (old + item_rate * (acc[...] - shrink * old)).astype(jnp.bfloat16)

    for n in hops:
        hops[n].wait_send()

    def sent(t, carry):
        relay(t).wait_send()
        return carry

    lax.fori_loop(0, UB - GROUP, sent, 0)
    lax.fori_loop(UB - GROUP + 1, UB, sent, 0)


def per_device(
    users, items, user_pairs, user_ratings, user_counts, item_pairs, item_ratings, live_item_counts
):
    bf, f32, i32 = jnp.bfloat16, jnp.float32, jnp.int32
    new_users, new_items = pl.pallas_call(
        kernel,
        out_shape=(
            pltpu.VMEM((UB, B, R), bf),
            pltpu.VMEM((IB, B, R), bf),
        ),
        in_specs=[pl.BlockSpec(memory_space=pl.ANY)] * 8,
        out_specs=(pl.BlockSpec(memory_space=pltpu.VMEM), pl.BlockSpec(memory_space=pltpu.VMEM)),
        scratch_shapes=[pltpu.VMEM((IB, B, R), bf)] * 8
        + [
            pltpu.VMEM((UB, B, R), bf),
            pltpu.VMEM((NS, CAP, B, B), bf),
            pltpu.VMEM((NSLOT + 1, B, B), bf),
            pltpu.VMEM((NSLOT + 1, B, R), f32),
            pltpu.VMEM((UB, B, R), bf),
            pltpu.VMEM((IB, B, R), f32),
            pltpu.SMEM((1, NS, CAP), i32),
            pltpu.SMEM((1, NS), i32),
            pltpu.SMEM((1,), i32),
            pltpu.VMEM((1, NS, CAP), i32),
            pltpu.VMEM((1, NSLOT), i32),
            pltpu.VMEM((8, 128), i32),
            pltpu.SMEM((8, 128), i32),
            pltpu.SemaphoreType.DMA((9,)),
            pltpu.SemaphoreType.DMA((NS,)),
            pltpu.SemaphoreType.DMA((14,)),
            pltpu.SemaphoreType.DMA((14,)),
            pltpu.SemaphoreType.DMA((UB,)),
            pltpu.SemaphoreType.DMA((UB,)),
            pltpu.SemaphoreType.REGULAR,
            pltpu.SemaphoreType.REGULAR,
        ],
        compiler_params=pltpu.CompilerParams(
            collective_id=0, has_side_effects=True, vmem_limit_bytes=VMEM
        ),
        name="round",
    )(
        users.reshape(UB, B, R), items.reshape(IB, B, R),
        user_pairs, user_ratings, user_counts, item_pairs, item_ratings, live_item_counts,
    )
    return new_users.reshape(users.shape), new_items.reshape(items.shape)


def solution(mesh):
    return jax.shard_map(
        per_device,
        mesh=mesh,
        in_specs=(
            P(("blk", "wide"), None),
            P(("blk", "wide"), None),
            P(("blk", "wide"), None, None),
            P(("blk", "wide"), None, None, None, None),
            P(("blk", "wide"), None),
            P(("blk", "wide"), None),
            P(("blk", "wide"), None, None, None),
            P(("blk", "wide")),
        ),
        out_specs=(P(("blk", "wide"), None), P(("blk", "wide"), None)),
        check_vma=False,
    )
```

```python
import jax
import jax.numpy as jnp
from jax import lax
from jax.experimental import pallas as pl
from jax.experimental.pallas import tpu as pltpu
from jax.sharding import PartitionSpec as P

MESH = pl.DeviceIdType.MESH

user_rate = 0.03
item_rate = 0.005
shrink = 0.05

B = 128
R = 256
UB = 32
IB = 4
NS = 8
CAP = 16
NSLOT = NS * CAP
VMEM = 61 * 2**20
LOCAL = 2**20
PIECES = 4
GROUP = 4
EARLY = 2
SENDS = ((3, 4, 5, 2, 6, 1, 7), (4, 3, 5, 2, 6, 1, 7))
TAKES = ((4, 3, 5, 2, 6, 1, 7), (4, 3, 5, 2, 6, 1, 7))

ORDER = ((0, 0), (0, 1), (0, 3), (1, 0), (0, 2), (1, 1), (1, 3), (1, 2))


def nt(a, b):
    return lax.dot_general(a, b, (((1,), (1,)), ((), ())), preferred_element_type=jnp.float32)


def nn(a, b):
    return lax.dot_general(a, b, (((1,), (0,)), ((), ())), preferred_element_type=jnp.float32)


def kernel(
    users, items, pairs, ratings, counts, ipairs, iratings, icount,
    nu_v, ni_v,
    h00, h01, h02, h03, h10, h11, h12, h13,
    users_v, ur_v, ir_v, terms, recv, acc,
    pairs_s, counts_s, icount_s, pairs_v, ipairs_v, tab_v, tab_s,
    lsem, ursem, gs, gr, ss, rs, token, entered,
):
    blk = lax.axis_index("blk")
    wide = lax.axis_index("wide")
    xh, y = lax.div(blk, 4), lax.rem(blk, 4)
    xl, z, core = lax.div(wide, 16), lax.rem(lax.div(wide, 2), 8), lax.rem(wide, 2)
    held = {(0, 0): h00, (0, 1): h01, (0, 2): h02, (0, 3): h03,
            (1, 0): h10, (1, 1): h11, (1, 2): h12, (1, 3): h13}

    def slice_of(fx, dy):
        return lax.rem(xh + fx, 2) * 4 + lax.rem(y + 4 - dy, 4)

    up = (xh * 4 + lax.rem(y + 1, 4), wide)
    down = (xh * 4 + lax.rem(y + 3, 4), wide)
    across = (lax.rem(blk + 4, 8), wide)

    def partner(t, sign):
        dz = lax.rem(lax.div(t, 4) + 1, 8)
        e = lax.rem(t, 4)
        xx = lax.rem(xl + lax.div(e, 2), 2)
        cc = lax.rem(core + lax.rem(e, 2), 2)
        zz = lax.rem(z + 8 + sign * dz, 8)
        return xx * 16 + zz * 2 + cc

    def slot(n, order):
        dz = 0
        for m in range(7):
            dz = jnp.where(n == m, jnp.where(z < 4, order[0][m], order[1][m]), dz)
        return (dz - 1) * 4

    place = z
    below = xl * 16 + lax.rem(z + 7, 8) * 2 + core
    above = xl * 16 + lax.rem(z + 1, 8) * 2 + core
    plane = (
        xl * 16 + z * 2 + 1 - core,
        (1 - xl) * 16 + z * 2 + core,
        (1 - xl) * 16 + z * 2 + 1 - core,
    )
    barrier = pltpu.get_barrier_semaphore()
    for dev in (up, down, across):
        pl.semaphore_signal(barrier, inc=1, device_id=dev, device_id_type=MESH)
    for dev in plane:
        pl.semaphore_signal(barrier, inc=1, device_id=(blk, dev), device_id_type=MESH)

    @pl.when(place > 0)
    def _():
        pl.semaphore_signal(barrier, inc=1, device_id=(blk, below), device_id_type=MESH)

    local = [
        pltpu.make_async_copy(items, h00, lsem.at[0]),
        pltpu.make_async_copy(pairs, pairs_v, lsem.at[1]),
        pltpu.make_async_copy(ipairs, ipairs_v, lsem.at[2]),
        pltpu.make_async_copy(pairs, pairs_s, lsem.at[3]),
        pltpu.make_async_copy(counts, counts_s, lsem.at[4]),
        pltpu.make_async_copy(icount, icount_s, lsem.at[5]),
        pltpu.make_async_copy(users, users_v, lsem.at[6]),
    ]
    for copy in local:
        copy.start()
    rating_copies = [
        pltpu.make_async_copy(ratings.at[0, slice_of(fx, dy)], ur_v.at[j], ursem.at[j])
        for j, (fx, dy) in enumerate(ORDER)
    ]
    rating_copies[0].start()
    irating_copy = pltpu.make_async_copy(iratings.at[0], ir_v.at[pl.ds(0, NSLOT)], lsem.at[7])

    pl.semaphore_wait(barrier, 6 + jnp.where(place < 7, 1, 0))

    def send(n, src, dst, dev):
        return pltpu.make_async_remote_copy(
            src_ref=src, dst_ref=dst, send_sem=gs.at[n], recv_sem=gr.at[n], device_id=dev, device_id_type=MESH
        )

    lo, hi = pl.ds(0, IB // 2), pl.ds(IB // 2, IB // 2)
    hops = {}

    def go(n, src, dst, half, dev):
        hops[n] = send(n, src.at[half], dst.at[half], dev)
        hops[n].start()

    go(0, items, h01, lo, up)
    go(1, items, h03, hi, down)
    go(2, items, h10, lo, across)
    go(3, items, h10, hi, across)
    go(4, items, h01, hi, up)
    go(5, items, h03, lo, down)
    for copy in rating_copies[1:]:
        copy.start()

    @pl.when(place > 0)
    def _():
        pl.semaphore_wait(token, 1)

    @pl.when(place < 7)
    def _():
        pl.semaphore_signal(token, inc=1, device_id=(blk, above), device_id_type=MESH)

    def greet(n, carry):
        e, zz = lax.rem(n, 4), lax.div(n, 4)
        dev = lax.div(e, 2) * 16 + zz * 2 + lax.rem(e, 2)
        pl.semaphore_signal(entered, inc=1, device_id=(blk, dev), device_id_type=MESH)
        return carry

    lax.fori_loop(0, 4 * place, greet, 0)

    terms[NSLOT] = jnp.zeros((B, R), jnp.float32)
    ir_v[NSLOT] = jnp.zeros((B, B), jnp.bfloat16)
    for n in (1, 2, 5):
        local[n].wait()
    sub = lax.broadcasted_iota(jnp.int32, (B, B), 0)
    lane = lax.broadcasted_iota(jnp.int32, (B, B), 1)
    k16 = lax.broadcasted_iota(jnp.int32, (CAP, B), 0)
    l16 = lax.broadcasted_iota(jnp.int32, (CAP, B), 1)
    spread = jnp.where(lax.rem(l16, CAP) == k16, jnp.float32(1), jnp.float32(0)).astype(jnp.bfloat16)
    wide_pairs = nn(pairs_v[0].astype(jnp.float32).astype(jnp.bfloat16), spread)
    s8 = lax.broadcasted_iota(jnp.int32, (NS, B), 0)
    j8 = lax.div(lax.broadcasted_iota(jnp.int32, (NS, B), 1), CAP)
    picked = jnp.zeros((NS, B), jnp.bool_)
    for j, (fx, dy) in enumerate(ORDER):
        picked = picked | ((j8 == j) & (s8 == slice_of(fx, dy)))
    pair_row = jnp.sum(jnp.where(picked, wide_pairs, 0.0), axis=0, keepdims=True)
    user_row = jnp.floor(pair_row * 0.25)
    user_here = jnp.broadcast_to(user_row, (B, B))
    user_there = user_here.T
    before = jnp.max(jnp.where((user_here == user_there) & (sub < lane), sub, -1), axis=0, keepdims=True)
    last = jnp.max(jnp.where(user_there == lane.astype(jnp.float32), sub, -1), axis=0, keepdims=True)
    item_row = jnp.broadcast_to(ipairs_v[...].astype(jnp.float32), (B, B)).T
    slot_of = jnp.min(
        jnp.where((item_row == lane.astype(jnp.float32)) & (sub < icount_s[0]), sub, NSLOT), axis=0, keepdims=True
    )
    tab_v[0:1, :] = jnp.where(before < 0, NSLOT, before)
    tab_v[1:2, :] = jnp.where(last < 0, NSLOT, last)
    tab_v[2:3, :] = slot_of
    tab_copy = pltpu.make_async_copy(tab_v, tab_s, lsem.at[8])
    tab_copy.start()
    for n in (3, 4, 6):
        local[n].wait()
    tab_copy.wait()

    def work(j):
        STEP = CAP if j == NS - 1 else 8
        fx, dy = ORDER[j]
        cols_ref = held[(fx, dy)]
        s = slice_of(fx, dy)
        rating_copies[j].wait()
        live = counts_s[0, s]

        def body(g, carry):
            cols, errs = [], []
            for e in range(STEP):
                k = g * STEP + e
                p = pairs_s[0, s, k]
                rows = users_v[lax.shift_right_logical(p, 2)]
                col = cols_ref[lax.bitwise_and(p, 3)]
                r = ur_v[j, k].astype(jnp.float32)
                seen = (r != 0) & (k < live)
                errs.append(jnp.where(seen, r - nt(rows, col), 0.0).astype(jnp.bfloat16))
                cols.append(col)
            for e in range(STEP):
                n = j * CAP + g * STEP + e
                terms[n] = terms[tab_s[0, n]] + nn(errs[e], cols[e])
            return carry

        lax.fori_loop(0, CAP // STEP, body, 0)

    local[0].wait()
    work(0)
    hops[0].wait_recv()
    go(6, h01, h02, lo, up)
    go(7, h01, h11, lo, across)
    hops[1].wait_recv()
    go(8, h03, h02, hi, down)
    go(9, h03, h13, hi, across)
    hops[2].wait_recv()
    hops[3].wait_recv()
    go(10, h10, h11, hi, up)
    go(11, h10, h13, lo, down)
    hops[4].wait_recv()
    work(1)
    hops[5].wait_recv()
    work(2)
    work(3)
    irating_copy.start()
    hops[6].wait_recv()
    hops[8].wait_recv()
    work(4)
    hops[7].wait_recv()
    go(12, h11, h12, lo, up)
    hops[9].wait_recv()
    go(13, h13, h12, hi, down)
    hops[10].wait_recv()
    work(5)
    hops[11].wait_recv()
    work(6)
    hops[12].wait_recv()
    hops[13].wait_recv()
    work(7)

    @pl.when(place < 7)
    def _():
        pl.semaphore_wait(entered, 4 * (7 - place))

    def update(u):
        old = users_v[u].astype(jnp.float32)
        total = terms[tab_s[1, u]]
        nu_v[u] = (old + user_rate * (total - shrink * old)).astype(jnp.bfloat16)

    def relay(t):
        u = partner(t, 1)
        return pltpu.make_async_remote_copy(
            src_ref=nu_v.at[u], dst_ref=recv.at[t], send_sem=ss.at[t], recv_sem=rs.at[t],
            device_id=(blk, u), device_id_type=MESH,
        )

    def send_out(n, carry):
        first = slot(n, SENDS)
        for e in range(GROUP):
            update(partner(first + e, 1))
            relay(first + e).start()
        return carry

    lax.fori_loop(0, EARLY, send_out, 0)
    for t in range(UB - GROUP + 1, UB):
        update(partner(t, 1))
        relay(t).start()
    lax.fori_loop(EARLY, UB // GROUP - 1, send_out, 0)
    update(wide)
    recv[UB - GROUP] = nu_v[wide]
    irating_copy.wait()
    acc[...] = jnp.zeros_like(acc)

    def absorb(t, owners):
        some = recv[pl.ds(t, GROUP)].reshape(GROUP * B, R)
        guess = nt(h00[...].reshape(IB * B, R), some)
        errs = []
        for i in range(IB):
            rate = jnp.concatenate([ir_v[tab_s[2, i * UB + u]] for u in owners], axis=1).astype(jnp.float32)
            errs.append(jnp.where(rate != 0, rate - guess[i * B : (i + 1) * B], 0.0).astype(jnp.bfloat16))
        acc[...] += nn(jnp.concatenate(errs, axis=0), some).reshape(IB, B, R)

    def take(n, carry):
        t = slot(n, TAKES)
        for e in range(GROUP):
            relay(t + e).wait_recv()
        absorb(t, [partner(t + e, -1) for e in range(GROUP)])
        return carry

    lax.fori_loop(0, EARLY, take, 0)
    t = UB - GROUP
    for e in range(1, GROUP):
        relay(t + e).wait_recv()
    absorb(t, [wide] + [partner(t + e, -1) for e in range(1, GROUP)])
    lax.fori_loop(EARLY, UB // GROUP - 1, take, 0)
    old = h00[...].astype(jnp.float32)
    ni_v[...] = (old + item_rate * (acc[...] - shrink * old)).astype(jnp.bfloat16)

    for n in hops:
        hops[n].wait_send()

    def sent(t, carry):
        relay(t).wait_send()
        return carry

    lax.fori_loop(0, UB - GROUP, sent, 0)
    lax.fori_loop(UB - GROUP + 1, UB, sent, 0)


def deliver(made_users, made_items, new_users, new_items, sem):
    copies = [pltpu.make_async_copy(made_items, new_items, sem.at[PIECES])]
    for n in range(PIECES):
        part = pl.ds(n * (UB // PIECES), UB // PIECES)
        copies.append(pltpu.make_async_copy(made_users.at[part], new_users.at[part], sem.at[n]))
    for copy in copies:
        copy.start()
    for copy in copies:
        copy.wait()


def per_device(
    users, items, user_pairs, user_ratings, user_counts, item_pairs, item_ratings, live_item_counts
):
    bf, f32, i32 = jnp.bfloat16, jnp.float32, jnp.int32
    made_users, made_items = pl.pallas_call(
        kernel,
        out_shape=(
            pltpu.VMEM((UB, B, R), bf),
            pltpu.VMEM((IB, B, R), bf),
        ),
        in_specs=[pl.BlockSpec(memory_space=pl.ANY)] * 8,
        out_specs=(pl.BlockSpec(memory_space=pltpu.VMEM), pl.BlockSpec(memory_space=pltpu.VMEM)),
        scratch_shapes=[pltpu.VMEM((IB, B, R), bf)] * 8
        + [
            pltpu.VMEM((UB, B, R), bf),
            pltpu.VMEM((NS, CAP, B, B), bf),
            pltpu.VMEM((NSLOT + 1, B, B), bf),
            pltpu.VMEM((NSLOT + 1, B, R), f32),
            pltpu.VMEM((UB, B, R), bf),
            pltpu.VMEM((IB, B, R), f32),
            pltpu.SMEM((1, NS, CAP), i32),
            pltpu.SMEM((1, NS), i32),
            pltpu.SMEM((1,), i32),
            pltpu.VMEM((1, NS, CAP), i32),
            pltpu.VMEM((1, NSLOT), i32),
            pltpu.VMEM((8, 128), i32),
            pltpu.SMEM((8, 128), i32),
            pltpu.SemaphoreType.DMA((9,)),
            pltpu.SemaphoreType.DMA((NS,)),
            pltpu.SemaphoreType.DMA((14,)),
            pltpu.SemaphoreType.DMA((14,)),
            pltpu.SemaphoreType.DMA((UB,)),
            pltpu.SemaphoreType.DMA((UB,)),
            pltpu.SemaphoreType.REGULAR,
            pltpu.SemaphoreType.REGULAR,
        ],
        compiler_params=pltpu.CompilerParams(
            collective_id=0, has_side_effects=True, vmem_limit_bytes=VMEM
        ),
        name="round",
    )(
        users.reshape(UB, B, R), items.reshape(IB, B, R),
        user_pairs, user_ratings, user_counts, item_pairs, item_ratings, live_item_counts,
    )
    new_users, new_items = pl.pallas_call(
        deliver,
        out_shape=(
            jax.ShapeDtypeStruct((UB, B, R), bf),
            jax.ShapeDtypeStruct((IB, B, R), bf),
        ),
        in_specs=[pl.BlockSpec(memory_space=pl.ANY)] * 2,
        out_specs=(pl.BlockSpec(memory_space=pl.ANY), pl.BlockSpec(memory_space=pl.ANY)),
        scratch_shapes=[pltpu.SemaphoreType.DMA((PIECES + 1,))],
        compiler_params=pltpu.CompilerParams(vmem_limit_bytes=LOCAL),
        name="deliver",
    )(made_users, made_items)
    return new_users.reshape(users.shape), new_items.reshape(items.shape)


def solution(mesh):
    return jax.shard_map(
        per_device,
        mesh=mesh,
        in_specs=(
            P(("blk", "wide"), None),
            P(("blk", "wide"), None),
            P(("blk", "wide"), None, None),
            P(("blk", "wide"), None, None, None, None),
            P(("blk", "wide"), None),
            P(("blk", "wide"), None),
            P(("blk", "wide"), None, None, None),
            P(("blk", "wide")),
        ),
        out_specs=(P(("blk", "wide"), None), P(("blk", "wide"), None)),
        check_vma=False,
    )
```
